32 devices in a mesh: expert: 4 (over z), tensor: 8 (over y, x, core).
Axes of the slice: x: 2, y: 2, z: 4, core: 2. Of those that a mesh axis runs over, the one named last changes fastest.
Arguments:
- activations: bfloat16 [3072, 512], P('tensor', 'expert'), may hold values from -6 to 6
- cotangent: bfloat16 [3072, 512], P('tensor', 'expert'), may hold values from -4 to 4
- route_ids: int32 [512, 2], P('expert'), may hold values from 0 to 3, all different within a row; in each aligned block of 128 rows (0 to 127, 128 to 255, ...) at most 80 rows name the same one
- gate_probs: float32 [512, 2], P('expert'), may hold values from 0.2 to 0.8
- gate_weight: bfloat16 [4, 3072, 16384], P('expert', None, 'tensor'), may hold values from -0.15625 to 0.15625
- up_weight: bfloat16 [4, 3072, 16384], P('expert', None, 'tensor'), may hold values from -0.15625 to 0.15625
- down_weight: bfloat16 [4, 16384, 3072], P('expert', 'tensor'), may hold values from -0.046875 to 0.046875
Outputs:
- grad_input: bfloat16 [3072, 512], P('tensor', 'expert')
- score_grad: float32 [512, 2], P('expert')
The draws below stay inside these ranges and needn't reach their ends.
Inputs may be any that keep to these rules, and one draw needn't show every extreme that they name: `route_ids`: each token names 2 different experts. Among the 128 tokens of one index of the expert axis no expert is named more than 80 times, and in every draw some such block names one expert exactly 80 times.
All inputs are finite; a program needn't handle non-finite values.
Results may differ from the reference program's by a relative error of at most 0.008.
Values may be sent and summed in bfloat16 or wider, within the bound.
A program may use at most 128 MiB of HBM per device.

```python
import math
import jax
import jax.numpy as jnp
import numpy as np
from jax import lax

D = 3072
FF = 16384
TOP = 2
TOK_GRP = 128
EXPERTS = 4
CAP = 80
ROWS = 320
TOKENS = 512


def raised(drawn, key, source, target, parts, factor):
    def block_of(dim):
        return (jnp.arange(drawn.shape[dim]) // (drawn.shape[dim] // parts)).reshape((-1,) + (1,) * (drawn.ndim - 1 - dim))

    one_side = jax.random.permutation(key, parts)[block_of(target)]
    far = (block_of(target) + parts // 2) % parts
    return jnp.where((block_of(source) == one_side) | (block_of(source) == far), factor * drawn, drawn)


def shard_levels(stream_key, shape, cuts, least, top_value):
    gain, own = 1.0, jax.random.fold_in(stream_key, 6)
    for dim, blocks in cuts:
        draws = jnp.exp(jax.random.uniform(jax.random.fold_in(own, dim), (blocks,), jnp.float32, least / len(cuts), top_value / len(cuts)))
        gain = gain * jnp.repeat(draws, shape[dim] // blocks).reshape([-1 if axis == dim else 1 for axis in range(len(shape))])
    return gain


def assign_block(key, own, number, rows, count, top, most, slope):
    sequence = jax.random.permutation(key, count)
    crowded, usual = load_shares(count, rows * top, most, slope, True), load_shares(count, rows * top, most, slope, False)
    places = jnp.arange(count)

    def named(sizes, rotation):
        used = int((sizes > 0).sum())
        fixed = max(1, used // 4)
        shifted = fixed + (places - fixed + rotation * (used - fixed)) % max(1, count - fixed)
        return jnp.zeros((count,), jnp.int32).at[sequence[jnp.where(places < fixed, places, shifted)]].set(jnp.asarray(sizes, jnp.int32))

    sizes = jnp.where(number % 4 == 0, named(crowded, number // 4), named(usual, number - number // 4 - 1))
    mixed = jax.random.permutation(jax.random.fold_in(own, 3), count)
    source_of, receiver = mixed[0:count // 2 * 2:2], mixed[1:count // 2 * 2:2]
    margin = jnp.minimum(sizes[source_of] - 1, most - sizes[receiver]) // 2
    margin = jnp.where((source_of == sequence[0]) | (receiver == sequence[0]) | (sizes[receiver] == 0), 0, jnp.maximum(margin, 0))
    shifted = jax.random.randint(jax.random.fold_in(own, 4), (count // 2,), 0, 1 << 20) % (margin + 1)
    sizes = sizes.at[source_of].add(-shifted).at[receiver].add(shifted)
    labels = jnp.searchsorted(jnp.cumsum(sizes), jnp.arange(rows * top), side="right").astype(jnp.int32)
    table = labels.reshape(top, rows).T
    table = table[jax.random.permutation(jax.random.fold_in(own, 1), rows)]
    rotation = jax.random.randint(jax.random.fold_in(own, 2), (rows, 1), 0, top)
    return jnp.take_along_axis(table, (jnp.arange(top)[None, :] + rotation) % top, axis=1)


def load_shares(amount, total, reach, skew, full):
    weights = [(1 << 20) // math.isqrt(grade ** skew) + 1 for grade in range(1, amount + 1)]
    largest = reach if full else min(reach, max(-(-total // amount), total * weights[0] // sum(weights)))
    least = 1 if total - largest >= amount - 1 else 0
    given, surplus = [largest] + [least] * (amount - 1), total - largest - least * (amount - 1)
    while surplus > 0:
        movable = [i for i in range(1, amount) if given[i] < largest] or [i for i in range(1, amount) if given[i] < reach]
        mass, left = sum([weights[i] for i in movable]), surplus
        for i in movable:
            addition = min(reach - given[i], max(1, left * weights[i] // mass), surplus)
            given[i] = given[i] + addition
            surplus = surplus - addition
    return np.array(given)


def normal_values(key, dims, width, reach, shards=(), kind=jnp.bfloat16):
    values = width * jax.random.normal(key, dims, jnp.float32)
    if shards:
        values = values * shard_levels(key, dims, shards, -0.22, 0.18)
    return jnp.clip(values, -reach, reach).astype(kind)


def heavy_noise(stream_key, shape, width, limit, shards, heavy, kind=jnp.bfloat16):
    drawn = width * jax.random.normal(stream_key, shape, jnp.float32)
    if shards:
        drawn = drawn * shard_levels(stream_key, shape, shards, -0.22, 0.18)
    return jnp.clip(raised(drawn, jax.random.fold_in(stream_key, 3), *heavy), -limit, limit).astype(kind)


def setup_inputs(seed: int = 0) -> dict:
    keys = jax.random.split(jax.random.key(seed), 8)
    activations = normal_values(keys[0], (D, TOKENS), 1.0, 6.0, ((0, 8), (1, 4)))
    cotangent = normal_values(keys[1], (D, TOKENS), 0.25, 4.0, ((0, 8), (1, 4)))
    route_ids_keys = jax.random.split(jax.random.fold_in(keys[2], 1), TOKENS // TOK_GRP)
    route_ids_turns = jax.random.permutation(jax.random.fold_in(keys[2], 3), TOKENS // TOK_GRP)
    route_ids = jax.vmap(lambda own, number: assign_block(jax.random.fold_in(keys[2], 2), own, number, TOK_GRP, EXPERTS, TOP, CAP, 2))(route_ids_keys, route_ids_turns).reshape((TOKENS, TOP))
    gate_probs = jnp.clip(0.2 + 0.6 * jax.random.uniform(keys[3], (TOKENS, TOP), jnp.float32) ** shard_levels(keys[3], (TOKENS, TOP), ((0, 4),), -0.2, 0.2), 0.2, 0.8)
    gate_weight = heavy_noise(keys[4], (EXPERTS, D, FF), D ** -0.5, 0.15625, ((0, 4), (2, 8)), (2, 1, 8, 2.0))
    up_weight = heavy_noise(keys[5], (EXPERTS, D, FF), D ** -0.5, 0.15625, ((0, 4), (2, 8)), (2, 1, 8, 2.0))
    down_weight = normal_values(keys[6], (EXPERTS, FF, D), FF ** -0.5, 0.046875, ((0, 4), (1, 8)))
    return {"activations": activations, "cotangent": cotangent, "route_ids": route_ids, "gate_probs": gate_probs, "gate_weight": gate_weight, "up_weight": up_weight, "down_weight": down_weight}


def swiglu_backward(gate_sum, up_sum, hidden_grad):
    sigma = jax.nn.sigmoid(gate_sum)
    silu_value = gate_sum * sigma
    grad_up = (hidden_grad * silu_value).astype(jnp.bfloat16)
    grad_gate = (hidden_grad * up_sum * sigma * (1.0 + gate_sum * (1.0 - sigma))).astype(jnp.bfloat16)
    score_rows = jnp.sum(silu_value * up_sum * hidden_grad, axis=1)
    return grad_gate, grad_up, score_rows


def reference(activations, cotangent, route_ids, gate_probs, gate_weight, up_weight, down_weight):
    features = activations.T
    output_grads = cotangent.T
    groups = TOKENS // TOK_GRP
    onehot = (route_ids[:, :, None] == jnp.arange(EXPERTS, dtype=jnp.int32)[None, None, :]).astype(jnp.int32)
    grouped = onehot.reshape(groups, TOK_GRP * TOP, EXPERTS)
    earlier = jnp.cumsum(grouped, axis=1) - grouped
    position = jnp.sum(earlier * grouped, axis=2).reshape(TOKENS, TOP)
    group_index = (jnp.arange(TOKENS, dtype=jnp.int32) // TOK_GRP)[:, None]
    row_index = (group_index * CAP + position).astype(jnp.int32)
    slot_range = jnp.arange(ROWS, dtype=jnp.int32)
    grad_total = jnp.zeros((TOKENS, D), jnp.float32)
    score_total = jnp.zeros((TOKENS, TOP), jnp.float32)
    for expert in range(EXPERTS):
        chosen = (route_ids == expert)[:, :, None] & (row_index[:, :, None] == slot_range[None, None, :])
        selection = jnp.sum(chosen.astype(jnp.float32), axis=1).astype(jnp.bfloat16)
        rows_in = jnp.dot(selection.T, features, preferred_element_type=jnp.float32).astype(jnp.bfloat16)
        rows_grad = jnp.dot(selection.T, output_grads, preferred_element_type=jnp.float32).astype(jnp.bfloat16)
        gate_sum = jnp.dot(rows_in, gate_weight[expert], preferred_element_type=jnp.float32)
        up_sum = jnp.dot(rows_in, up_weight[expert], preferred_element_type=jnp.float32)
        hidden_grad = jnp.dot(rows_grad, down_weight[expert].T, preferred_element_type=jnp.float32)
        grad_gate, grad_up, score_rows = swiglu_backward(gate_sum, up_sum, hidden_grad)
        terms = jnp.dot(grad_gate, gate_weight[expert].T, preferred_element_type=jnp.float32)
        terms = terms + jnp.dot(grad_up, up_weight[expert].T, preferred_element_type=jnp.float32)
        weighting = jnp.sum(jnp.where(chosen, gate_probs[:, :, None], jnp.float32(0.0)), axis=1)
        grad_total = grad_total + jnp.dot(weighting, terms, precision=lax.Precision.HIGHEST, preferred_element_type=jnp.float32)
        score_total = score_total + jnp.sum(jnp.where(chosen, score_rows[None, None, :], jnp.float32(0.0)), axis=2)
    return grad_total.T.astype(jnp.bfloat16), score_total
```

```python
import jax
import jax.numpy as jnp
from jax import lax
from jax.sharding import PartitionSpec as P


EXTRA_ROWS = 16


def slot_numbers(route_ids, expert_count, capacity):
    token_count = route_ids.shape[0]
    onehot = route_ids[:, :, None] == jnp.arange(expert_count, dtype=jnp.int32)[None, None, :]
    named = jnp.sum(onehot.astype(jnp.float32), axis=1).astype(jnp.bfloat16)
    order = jnp.arange(token_count, dtype=jnp.int32)
    before = (order[None, :] < order[:, None]).astype(jnp.bfloat16)
    earlier = jnp.dot(before, named, preferred_element_type=jnp.float32)
    position = jnp.sum(jnp.where(onehot, earlier[:, None, :], 0.0), axis=2).astype(jnp.int32)
    return route_ids * capacity + position


def swiglu_backward(gate_sum, up_sum, hidden_grad):
    sigma = jax.nn.sigmoid(gate_sum)
    silu_value = gate_sum * sigma
    grad_up = (hidden_grad * silu_value).astype(jnp.bfloat16)
    grad_gate = (hidden_grad * up_sum * sigma * (1.0 + gate_sum * (1.0 - sigma))).astype(
        jnp.bfloat16
    )
    score_rows = jnp.sum(silu_value * up_sum * hidden_grad, axis=1)
    return (grad_gate, grad_up, score_rows)


def body(activations, cotangent, route_ids, gate_probs, gate_weight, up_weight, down_weight):
    expert_count = lax.axis_size("expert")
    tokens_here = route_ids.shape[0]
    capacity = min(tokens_here, 5 * tokens_here // (2 * expert_count))
    slot_total = expert_count * capacity
    destination = slot_numbers(route_ids, expert_count, capacity)
    slot_range = jnp.arange(slot_total, dtype=jnp.int32)
    matches = destination[:, :, None] == slot_range[None, None, :]
    placing = jnp.sum(matches.astype(jnp.float32), axis=1).astype(jnp.bfloat16)
    weighting = jnp.sum(jnp.where(matches, gate_probs[:, :, None], jnp.float32(0.0)), axis=1)
    gate_local = gate_weight[0]
    up_local = up_weight[0]
    down_local = down_weight[0]
    first_dims = (((0,), (0,)), ((), ()))
    down_dims = (((0,), (1,)), ((), ()))
    hidden_dims = (((1,), (1,)), ((), ()))
    features_here = activations.shape[0]
    both = jnp.concatenate([activations, cotangent], axis=0)
    send = jnp.dot(both, placing, preferred_element_type=jnp.float32).astype(jnp.bfloat16)
    recv = lax.all_to_all(send, "expert", split_axis=1, concat_axis=1, tiled=True)
    recv_in, recv_grad = recv[:features_here], recv[features_here:]
    feature_piece = lax.all_gather(recv_in, "tensor", axis=0, tiled=True)
    grad_piece = lax.all_gather(recv_grad, "tensor", axis=0, tiled=True)
    gate_rows = gate_local
    up_rows = up_local
    gate_sum = lax.dot_general(
        feature_piece, gate_rows, first_dims, preferred_element_type=jnp.float32
    )
    up_sum = lax.dot_general(feature_piece, up_rows, first_dims, preferred_element_type=jnp.float32)
    hidden_grad = lax.dot_general(
        grad_piece, down_local, down_dims, preferred_element_type=jnp.float32
    )
    gate_sum, up_sum, hidden_grad = (gate_sum, up_sum, hidden_grad)
    grad_gate, grad_up, score_rows = swiglu_backward(gate_sum, up_sum, hidden_grad)
    gate_rows = gate_local
    up_rows = up_local
    term = lax.dot_general(gate_rows, grad_gate, hidden_dims, preferred_element_type=jnp.float32)
    term = term + lax.dot_general(
        up_rows, grad_up, hidden_dims, preferred_element_type=jnp.float32
    )
    tensor_count = lax.axis_size("tensor")
    score_high = score_rows.astype(jnp.bfloat16)
    score_low = (score_rows - score_high.astype(jnp.float32)).astype(jnp.bfloat16)
    extra = jnp.concatenate(
        [
            score_high[None, :],
            score_low[None, :],
            jnp.zeros((EXTRA_ROWS - 2, slot_total), jnp.bfloat16),
        ],
        axis=0,
    )
    blocks = term.astype(jnp.bfloat16).reshape(tensor_count, features_here, slot_total)
    extra = jnp.broadcast_to(extra[None], (tensor_count, EXTRA_ROWS, slot_total))
    summed = lax.psum_scatter(
        jnp.concatenate([blocks, extra], axis=1), "tensor", scatter_dimension=0, tiled=False
    )
    back = lax.all_to_all(summed, "expert", split_axis=1, concat_axis=1, tiled=True)
    back = back.astype(jnp.float32)
    back_terms = back[:features_here]
    back_scores = back[features_here : features_here + 1] + back[features_here + 1 : features_here + 2]
    grad_local = jnp.dot(
        back_terms, weighting.T, precision=lax.Precision.HIGHEST, preferred_element_type=jnp.float32
    )
    score_grad = jnp.sum(
        jnp.where(matches, back_scores[0][None, None, :], jnp.float32(0.0)), axis=2
    )
    grad_input = grad_local.astype(jnp.bfloat16)
    return (grad_input, score_grad)


def solution(mesh):
    in_specs = (
        P("tensor", "expert"),
        P("tensor", "expert"),
        P("expert", None),
        P("expert", None),
        P("expert", None, "tensor"),
        P("expert", None, "tensor"),
        P("expert", "tensor", None),
    )
    out_specs = (P("tensor", "expert"), P("expert", None))
    return jax.shard_map(body, mesh=mesh, in_specs=in_specs, out_specs=out_specs, check_vma=False)
```

```python
import jax
import jax.numpy as jnp
from jax import lax
from jax.sharding import PartitionSpec as P


EXTRA_ROWS = 8


def slot_numbers(route_ids, expert_count, capacity):
    token_count = route_ids.shape[0]
    onehot = route_ids[:, :, None] == jnp.arange(expert_count, dtype=jnp.int32)[None, None, :]
    named = jnp.sum(onehot.astype(jnp.float32), axis=1).astype(jnp.bfloat16)
    order = jnp.arange(token_count, dtype=jnp.int32)
    before = (order[None, :] < order[:, None]).astype(jnp.bfloat16)
    earlier = jnp.dot(before, named, preferred_element_type=jnp.float32)
    position = jnp.sum(jnp.where(onehot, earlier[:, None, :], 0.0), axis=2).astype(jnp.int32)
    return route_ids * capacity + position


def swiglu_backward(gate_sum, up_sum, hidden_grad):
    sigma = jax.nn.sigmoid(gate_sum)
    silu_value = gate_sum * sigma
    grad_up = (hidden_grad * silu_value).astype(jnp.bfloat16)
    grad_gate = (hidden_grad * up_sum * sigma * (1.0 + gate_sum * (1.0 - sigma))).astype(
        jnp.bfloat16
    )
    score_rows = jnp.sum(silu_value * up_sum * hidden_grad, axis=1)
    return (grad_gate, grad_up, score_rows)


def body(activations, cotangent, route_ids, gate_probs, gate_weight, up_weight, down_weight):
    expert_count = lax.axis_size("expert")
    tokens_here = route_ids.shape[0]
    capacity = min(tokens_here, 5 * tokens_here // (2 * expert_count))
    slot_total = expert_count * capacity
    destination = slot_numbers(route_ids, expert_count, capacity)
    slot_range = jnp.arange(slot_total, dtype=jnp.int32)
    matches = destination[:, :, None] == slot_range[None, None, :]
    placing = jnp.sum(matches.astype(jnp.float32), axis=1).astype(jnp.bfloat16)
    weighting = jnp.sum(jnp.where(matches, gate_probs[:, :, None], jnp.float32(0.0)), axis=1)
    gate_local = gate_weight[0]
    up_local = up_weight[0]
    down_local = down_weight[0]
    first_dims = (((0,), (0,)), ((), ()))
    down_dims = (((0,), (1,)), ((), ()))
    hidden_dims = (((1,), (1,)), ((), ()))
    features_here = activations.shape[0]
    send_in = jnp.dot(activations, placing, preferred_element_type=jnp.float32).astype(jnp.bfloat16)
    send_grad = jnp.dot(cotangent, placing, preferred_element_type=jnp.float32).astype(jnp.bfloat16)
    recv_in, recv_grad = (
        lax.all_to_all(send_in, "expert", split_axis=1, concat_axis=1, tiled=True),
        lax.all_to_all(send_grad, "expert", split_axis=1, concat_axis=1, tiled=True),
    )
    feature_piece = lax.all_gather(recv_in, "tensor", axis=0, tiled=True)
    grad_piece = lax.all_gather(recv_grad, "tensor", axis=0, tiled=True)
    gate_rows = gate_local
    up_rows = up_local
    gate_sum = lax.dot_general(
        feature_piece, gate_rows, first_dims, preferred_element_type=jnp.float32
    )
    up_sum = lax.dot_general(feature_piece, up_rows, first_dims, preferred_element_type=jnp.float32)
    hidden_grad = lax.dot_general(
        grad_piece, down_local, down_dims, preferred_element_type=jnp.float32
    )
    gate_sum, up_sum, hidden_grad = (gate_sum, up_sum, hidden_grad)
    grad_gate, grad_up, score_rows = swiglu_backward(gate_sum, up_sum, hidden_grad)
    gate_rows = gate_local
    up_rows = up_local
    term = lax.dot_general(gate_rows, grad_gate, hidden_dims, preferred_element_type=jnp.float32)
    term = term + lax.dot_general(
        up_rows, grad_up, hidden_dims, preferred_element_type=jnp.float32
    )
    tensor_count = lax.axis_size("tensor")
    blocks = term.reshape(tensor_count, features_here, slot_total)
    extra = jnp.broadcast_to(score_rows[None, None, :], (tensor_count, EXTRA_ROWS, slot_total))
    summed = lax.psum_scatter(
        jnp.concatenate([blocks, extra], axis=1), "tensor", scatter_dimension=0, tiled=False
    )
    back = lax.all_to_all(summed, "expert", split_axis=1, concat_axis=1, tiled=True)
    back_terms = back[:features_here]
    back_scores = back[features_here : features_here + 1]
    grad_local = jnp.dot(
        back_terms, weighting.T, precision=lax.Precision.HIGHEST, preferred_element_type=jnp.float32
    )
    score_grad = jnp.sum(
        jnp.where(matches, back_scores[0][None, None, :], jnp.float32(0.0)), axis=2
    )
    grad_input = grad_local.astype(jnp.bfloat16)
    return (grad_input, score_grad)


def solution(mesh):
    in_specs = (
        P("tensor", "expert"),
        P("tensor", "expert"),
        P("expert", None),
        P("expert", None),
        P("expert", None, "tensor"),
        P("expert", None, "tensor"),
        P("expert", "tensor", None),
    )
    out_specs = (P("tensor", "expert"), P("expert", None))
    return jax.shard_map(body, mesh=mesh, in_specs=in_specs, out_specs=out_specs, check_vma=False)
```

```python
import jax
import jax.numpy as jnp
from jax import lax
from jax.sharding import PartitionSpec as P


EXTRA_ROWS = 16


def slot_numbers(route_ids, expert_count, capacity):
    token_count = route_ids.shape[0]
    onehot = route_ids[:, :, None] == jnp.arange(expert_count, dtype=jnp.int32)[None, None, :]
    named = jnp.sum(onehot.astype(jnp.float32), axis=1).astype(jnp.bfloat16)
    order = jnp.arange(token_count, dtype=jnp.int32)
    before = (order[None, :] < order[:, None]).astype(jnp.bfloat16)
    earlier = jnp.dot(before, named, preferred_element_type=jnp.float32)
    position = jnp.sum(jnp.where(onehot, earlier[:, None, :], 0.0), axis=2).astype(jnp.int32)
    return route_ids * capacity + position


def swiglu_backward(gate_sum, up_sum, hidden_grad):
    sigma = jax.nn.sigmoid(gate_sum)
    silu_value = gate_sum * sigma
    grad_up = (hidden_grad * silu_value).astype(jnp.bfloat16)
    grad_gate = (hidden_grad * up_sum * sigma * (1.0 + gate_sum * (1.0 - sigma))).astype(
        jnp.bfloat16
    )
    score_rows = jnp.sum(silu_value * up_sum * hidden_grad, axis=1)
    return (grad_gate, grad_up, score_rows)


def body(activations, cotangent, route_ids, gate_probs, gate_weight, up_weight, down_weight):
    expert_count = lax.axis_size("expert")
    tokens_here = route_ids.shape[0]
    capacity = min(tokens_here, 5 * tokens_here // (2 * expert_count))
    slot_total = expert_count * capacity
    destination = slot_numbers(route_ids, expert_count, capacity)
    slot_range = jnp.arange(slot_total, dtype=jnp.int32)
    matches = destination[:, :, None] == slot_range[None, None, :]
    placing = jnp.sum(matches.astype(jnp.float32), axis=1).astype(jnp.bfloat16)
    weighting = jnp.sum(jnp.where(matches, gate_probs[:, :, None], jnp.float32(0.0)), axis=1)
    gate_local = gate_weight[0]
    up_local = up_weight[0]
    down_local = down_weight[0]
    first_dims = (((0,), (0,)), ((), ()))
    down_dims = (((0,), (1,)), ((), ()))
    hidden_dims = (((1,), (1,)), ((), ()))
    features_here = activations.shape[0]
    send_in = jnp.dot(activations, placing, preferred_element_type=jnp.float32).astype(jnp.bfloat16)
    send_grad = jnp.dot(cotangent, placing, preferred_element_type=jnp.float32).astype(jnp.bfloat16)
    recv_in, recv_grad = (
        lax.all_to_all(send_in, "expert", split_axis=1, concat_axis=1, tiled=True),
        lax.all_to_all(send_grad, "expert", split_axis=1, concat_axis=1, tiled=True),
    )
    feature_piece = lax.all_gather(recv_in, "tensor", axis=0, tiled=True)
    grad_piece = lax.all_gather(recv_grad, "tensor", axis=0, tiled=True)
    gate_rows = gate_local
    up_rows = up_local
    gate_sum = lax.dot_general(
        feature_piece, gate_rows, first_dims, preferred_element_type=jnp.float32
    )
    up_sum = lax.dot_general(feature_piece, up_rows, first_dims, preferred_element_type=jnp.float32)
    hidden_grad = lax.dot_general(
        grad_piece, down_local, down_dims, preferred_element_type=jnp.float32
    )
    gate_sum, up_sum, hidden_grad = (gate_sum, up_sum, hidden_grad)
    grad_gate, grad_up, score_rows = swiglu_backward(gate_sum, up_sum, hidden_grad)
    gate_rows = gate_local
    up_rows = up_local
    term = lax.dot_general(gate_rows, grad_gate, hidden_dims, preferred_element_type=jnp.float32)
    term = term + lax.dot_general(
        up_rows, grad_up, hidden_dims, preferred_element_type=jnp.float32
    )
    tensor_count = lax.axis_size("tensor")
    score_high = score_rows.astype(jnp.bfloat16)
    score_low = (score_rows - score_high.astype(jnp.float32)).astype(jnp.bfloat16)
    extra = jnp.concatenate(
        [
            score_high[None, :],
            score_low[None, :],
            jnp.zeros((EXTRA_ROWS - 2, slot_total), jnp.bfloat16),
        ],
        axis=0,
    )
    blocks = term.astype(jnp.bfloat16).reshape(tensor_count, features_here, slot_total)
    extra = jnp.broadcast_to(extra[None], (tensor_count, EXTRA_ROWS, slot_total))
    parts = lax.all_to_all(
        jnp.concatenate([blocks, extra], axis=1), "tensor", split_axis=0, concat_axis=0, tiled=True
    ).astype(jnp.float32)
    totals = jnp.sum(parts, axis=0)
    score = totals[features_here : features_here + 1] + totals[features_here + 1 : features_here + 2]
    score_high = score.astype(jnp.bfloat16)
    score_low = (score - score_high.astype(jnp.float32)).astype(jnp.bfloat16)
    summed = jnp.concatenate(
        [
            totals[:features_here].astype(jnp.bfloat16),
            score_high,
            score_low,
            jnp.zeros((EXTRA_ROWS - 2, slot_total), jnp.bfloat16),
        ],
        axis=0,
    )
    back = lax.all_to_all(summed, "expert", split_axis=1, concat_axis=1, tiled=True)
    back = back.astype(jnp.float32)
    back_terms = back[:features_here]
    back_scores = back[features_here : features_here + 1] + back[features_here + 1 : features_here + 2]
    grad_local = jnp.dot(
        back_terms, weighting.T, precision=lax.Precision.HIGHEST, preferred_element_type=jnp.float32
    )
    score_grad = jnp.sum(
        jnp.where(matches, back_scores[0][None, None, :], jnp.float32(0.0)), axis=2
    )
    grad_input = grad_local.astype(jnp.bfloat16)
    return (grad_input, score_grad)


def solution(mesh):
    in_specs = (
        P("tensor", "expert"),
        P("tensor", "expert"),
        P("expert", None),
        P("expert", None),
        P("expert", None, "tensor"),
        P("expert", None, "tensor"),
        P("expert", "tensor", None),
    )
    out_specs = (P("tensor", "expert"), P("expert", None))
    return jax.shard_map(body, mesh=mesh, in_specs=in_specs, out_specs=out_specs, check_vma=False)
```

```python
import jax
import jax.numpy as jnp
from jax import lax
from jax.experimental import pallas as pl
from jax.experimental.pallas import tpu as pltpu
from jax.sharding import PartitionSpec as P


EXTRA_ROWS = 16


def slot_numbers(route_ids, expert_count, capacity):
    token_count = route_ids.shape[0]
    onehot = route_ids[:, :, None] == jnp.arange(expert_count, dtype=jnp.int32)[None, None, :]
    named = jnp.sum(onehot.astype(jnp.float32), axis=1).astype(jnp.bfloat16)
    order = jnp.arange(token_count, dtype=jnp.int32)
    before = (order[None, :] < order[:, None]).astype(jnp.bfloat16)
    earlier = jnp.dot(before, named, preferred_element_type=jnp.float32)
    position = jnp.sum(jnp.where(onehot, earlier[:, None, :], 0.0), axis=2).astype(jnp.int32)
    return route_ids * capacity + position


def hidden_kernel(gate_sum, up_sum, grads, gate, up, down, out, total, score):
    step = pl.program_id(0)
    blocks, features = total.shape[0], total.shape[1]

    @pl.when(step == 0)
    def _():
        total[...] = jnp.zeros_like(total)
        score[...] = jnp.zeros_like(score)

    hidden_grad = jnp.dot(down[...], grads[...], preferred_element_type=jnp.float32)
    a, b = gate_sum[...], up_sum[...]
    sigma = jax.nn.sigmoid(a)
    silu_value = a * sigma
    grad_up = (hidden_grad * silu_value).astype(jnp.bfloat16)
    grad_gate = (hidden_grad * b * sigma * (1.0 + a * (1.0 - sigma))).astype(jnp.bfloat16)
    score[...] += jnp.sum(silu_value * b * hidden_grad, axis=0, keepdims=True)

    @pl.loop(0, blocks)
    def _(block):
        rows = pl.ds(pl.multiple_of(block * features, features), features)
        total[block] += jnp.dot(
            gate[rows, :], grad_gate, preferred_element_type=jnp.float32
        ) + jnp.dot(up[rows, :], grad_up, preferred_element_type=jnp.float32)

    @pl.when(step == pl.num_programs(0) - 1)
    def _():
        high = score[...].astype(jnp.bfloat16).astype(jnp.float32)
        low = score[...] - high
        row = lax.broadcasted_iota(jnp.int32, (EXTRA_ROWS, score.shape[1]), 0)
        extra = jnp.where(row == 0, high, jnp.where(row == 1, low, 0.0)).astype(jnp.bfloat16)

        @pl.loop(0, blocks)
        def _(block):
            out[block, :features, :] = total[block].astype(jnp.bfloat16)
            out[block, features:, :] = extra


def hidden_terms(gate_sum, up_sum, grads, gate, up, down, blocks):
    hidden, slots = gate_sum.shape
    depth = grads.shape[0]
    tile = min(hidden, 256)
    features = depth // blocks
    return pl.pallas_call(
        hidden_kernel,
        grid=(hidden // tile,),
        in_specs=[
            pl.BlockSpec((tile, slots), lambda i: (i, 0)),
            pl.BlockSpec((tile, slots), lambda i: (i, 0)),
            pl.BlockSpec((depth, slots), lambda i: (0, 0)),
            pl.BlockSpec((depth, tile), lambda i: (0, i)),
            pl.BlockSpec((depth, tile), lambda i: (0, i)),
            pl.BlockSpec((tile, depth), lambda i: (i, 0)),
        ],
        out_specs=pl.BlockSpec((blocks, features + EXTRA_ROWS, slots), lambda i: (0, 0, 0)),
        out_shape=jax.ShapeDtypeStruct((blocks, features + EXTRA_ROWS, slots), jnp.bfloat16),
        scratch_shapes=[
            pltpu.VMEM((blocks, features, slots), jnp.float32),
            pltpu.VMEM((1, slots), jnp.float32),
        ],
        compiler_params=pltpu.CompilerParams(vmem_limit_bytes=48 * 2**20),
        cost_estimate=pl.CostEstimate(
            flops=6 * hidden * depth * slots,
            bytes_accessed=6 * hidden * depth,
            transcendentals=hidden * slots,
        ),
    )(gate_sum, up_sum, grads, gate, up, down)


def body(activations, cotangent, route_ids, gate_probs, gate_weight, up_weight, down_weight):
    expert_count = lax.axis_size("expert")
    tokens_here = route_ids.shape[0]
    capacity = min(tokens_here, 5 * tokens_here // (2 * expert_count))
    slot_total = expert_count * capacity
    destination = slot_numbers(route_ids, expert_count, capacity)
    slot_range = jnp.arange(slot_total, dtype=jnp.int32)
    matches = destination[:, :, None] == slot_range[None, None, :]
    placing = jnp.sum(matches.astype(jnp.float32), axis=1).astype(jnp.bfloat16)
    weighting = jnp.sum(jnp.where(matches, gate_probs[:, :, None], jnp.float32(0.0)), axis=1)
    gate_local = gate_weight[0]
    up_local = up_weight[0]
    down_local = down_weight[0]
    first_dims = (((0,), (0,)), ((), ()))
    features_here = activations.shape[0]
    send_in = jnp.dot(activations, placing, preferred_element_type=jnp.float32).astype(jnp.bfloat16)
    send_grad = jnp.dot(cotangent, placing, preferred_element_type=jnp.float32).astype(jnp.bfloat16)
    recv_in, recv_grad = (
        lax.all_to_all(send_in, "expert", split_axis=1, concat_axis=1, tiled=True),
        lax.all_to_all(send_grad, "expert", split_axis=1, concat_axis=1, tiled=True),
    )
    feature_piece = lax.all_gather(recv_in, "tensor", axis=0, tiled=True)
    grad_piece = lax.all_gather(recv_grad, "tensor", axis=0, tiled=True)
    gate_sum = lax.dot_general(
        gate_local, feature_piece, first_dims, preferred_element_type=jnp.float32
    )
    up_sum = lax.dot_general(up_local, feature_piece, first_dims, preferred_element_type=jnp.float32)
    terms = hidden_terms(
        gate_sum, up_sum, grad_piece, gate_local, up_local, down_local, lax.axis_size("tensor")
    )
    parts = lax.all_to_all(terms, "tensor", split_axis=0, concat_axis=0, tiled=True)
    parts = parts.astype(jnp.float32)
    totals = jnp.sum(parts, axis=0)
    score = totals[features_here : features_here + 1] + totals[features_here + 1 : features_here + 2]
    score_high = score.astype(jnp.bfloat16)
    score_low = (score - score_high.astype(jnp.float32)).astype(jnp.bfloat16)
    summed = jnp.concatenate(
        [
            totals[:features_here].astype(jnp.bfloat16),
            score_high,
            score_low,
            jnp.zeros((EXTRA_ROWS - 2, slot_total), jnp.bfloat16),
        ],
        axis=0,
    )
    back = lax.all_to_all(summed, "expert", split_axis=1, concat_axis=1, tiled=True)
    back = back.astype(jnp.float32)
    back_terms = back[:features_here]
    back_scores = back[features_here : features_here + 1] + back[features_here + 1 : features_here + 2]
    grad_local = jnp.dot(
        back_terms, weighting.T, precision=lax.Precision.HIGHEST, preferred_element_type=jnp.float32
    )
    score_grad = jnp.sum(
        jnp.where(matches, back_scores[0][None, None, :], jnp.float32(0.0)), axis=2
    )
    grad_input = grad_local.astype(jnp.bfloat16)
    return (grad_input, score_grad)


def solution(mesh):
    in_specs = (
        P("tensor", "expert"),
        P("tensor", "expert"),
        P("expert", None),
        P("expert", None),
        P("expert", None, "tensor"),
        P("expert", None, "tensor"),
        P("expert", "tensor", None),
    )
    out_specs = (P("tensor", "expert"), P("expert", None))
    return jax.shard_map(body, mesh=mesh, in_specs=in_specs, out_specs=out_specs, check_vma=False)
```
